32 devices in a mesh: rec: 8 (over y, x, core), rot: 4 (over z).
Axes of the slice: x: 2, y: 2, z: 4, core: 2. Of those that a mesh axis runs over, the one named last changes fastest.
Arguments:
- receptors: bfloat16 [64, 60, 900], P('rec'), may hold values from -0.09375 to 0.09375
- ligands: bfloat16 [64, 60, 900], P('rec'), may hold values from -6 to 6
- wigner: bfloat16 [32, 35990], P('rot')
- trans_table: bfloat16 [16, 30, 30, 30], replicated, may hold values from -1 to 1
- dist_index: int32 [8], replicated, may hold values from 0 to 15, as said below
Outputs:
- energy: float32 [64, 64], P('rec', 'rot')
The draws below stay inside these ranges and needn't reach their ends.
Inputs may be any that keep to these rules, and one draw needn't show every extreme that they name: `dist_index`: indices into the tabulated distances; the first and the last tabulated distance are both among them.
All inputs are finite; a program needn't handle non-finite values.
Results may differ from the reference program's by a relative error of at most 0.0035.
Values may be sent and summed in bfloat16 or wider, within the bound.
A program may use at most 192 MiB of HBM per device.

```python
import math
import jax
import jax.numpy as jnp
import numpy as np
from jax import lax

ORDER = 30
NRAD = 30
PROPS = 2
DISTS = 8
NTAB = 16
RECEPTORS = 64
LIGANDS = 64
ROTATIONS = 32
ANGULAR = 900
WPACK = 35990


def draw_wigner(key, part):
    degrees = np.concatenate([np.full((2 * degree + 1) ** 2, degree) for degree in range(ORDER)])
    scales = jnp.asarray(1.0 / np.sqrt(2.0 * degrees + 1.0), jnp.float32)
    values = jax.random.normal(key, (ROTATIONS, WPACK), jnp.float32)
    return (values * scales[None, :]).astype(jnp.bfloat16)


def draw_dist_index(key, part):
    picks = jax.random.randint(jax.random.fold_in(key, 1), (DISTS,), 0, NTAB)
    spots = jax.random.permutation(jax.random.fold_in(key, 2), DISTS)
    places = jnp.arange(DISTS)
    picks = jnp.where(places == spots[0], 0, picks)
    picks = jnp.where(places == spots[1], NTAB - 1, picks)
    return picks.astype(jnp.int32)


def block_levels(rng, dims, cuts, low, high):
    level = 1.0
    for position, blocks in cuts:
        steps = jax.random.uniform(jax.random.fold_in(jax.random.fold_in(rng, 6), position), (blocks,), jnp.float32, low / len(cuts), high / len(cuts))
        level = level * jnp.repeat(jnp.exp(steps), dims[position] // blocks).reshape((-1,) + (1,) * (len(dims) - 1 - position))
    return level


def centred(key, dims, spread, most, cuts=(), kind=jnp.bfloat16):
    level = block_levels(key, dims, cuts, -0.22, 0.18) if cuts else 1.0
    result = jax.random.normal(key, dims, jnp.float32) * spread * level
    return jnp.minimum(jnp.maximum(result, -most), most).astype(kind)


def setup_inputs(seed: int = 0) -> dict:
    streams_of = jax.random.split(jax.random.key(seed), 6)
    return {
        "receptors": centred(streams_of[0], (RECEPTORS, PROPS * NRAD, ANGULAR), (1.5 / (PROPS * NRAD * ANGULAR) ** 0.5), 0.09375, ((0, 8),)),
        "ligands": centred(streams_of[1], (LIGANDS, PROPS * NRAD, ANGULAR), 1.0, 6.0, ((0, 8),)),
        "wigner": draw_wigner(jax.random.fold_in(streams_of[5], 71), 0),
        "trans_table": centred(streams_of[3], (NTAB, ORDER, NRAD, NRAD), NRAD ** -0.5, 1.0),
        "dist_index": draw_dist_index(jax.random.fold_in(streams_of[5], 71), 0),
    }


def packed_start(degree):
    return degree * (4 * degree * degree - 1) // 3

def translate(coeffs, tables):
    numrows = coeffs.shape[0]
    radial = tables.shape[2]
    split_rows = coeffs.reshape(numrows, coeffs.shape[1] // radial, radial, coeffs.shape[2]).astype(jnp.float32)
    pieces = []
    for degree in range(tables.shape[1]):
        column_lo = degree * degree
        extent = 2 * degree + 1
        window = split_rows[..., column_lo:column_lo + extent]
        pieces.append(jnp.einsum('tji,rpic->trpjc', tables[:, degree].astype(jnp.float32), window))
    joined = jnp.concatenate(pieces, axis=-1)
    return joined.reshape(tables.shape[0], numrows, coeffs.shape[1], coeffs.shape[2]).astype(jnp.bfloat16)

def rotate(coeffs, wigner):
    angular = coeffs.shape[2]
    degrees = math.isqrt(angular)
    pieces = []
    for degree in range(degrees):
        extent = 2 * degree + 1
        offset = packed_start(degree)
        window = coeffs[..., degree * degree:degree * degree + extent].astype(jnp.float32)
        matrix = wigner[:, offset:offset + extent * extent].reshape(wigner.shape[0], extent, extent).astype(jnp.float32)
        pieces.append(jnp.einsum('gxm,qmk->qgxk', window, matrix))
    return jnp.concatenate(pieces, axis=-1).astype(jnp.bfloat16)

def weight_sums(translated, rotated):
    width_all = translated.shape[2] * translated.shape[3]
    left_rows = translated.reshape(-1, width_all)
    right_rows = rotated.reshape(-1, width_all)
    score = jnp.dot(left_rows, right_rows.T, preferred_element_type=jnp.float32)
    weights = jnp.exp(score).reshape(translated.shape[0], translated.shape[1], rotated.shape[0], rotated.shape[1])
    return lax.optimization_barrier(jnp.sum(weights, axis=(0, 2)))

def reference(receptors, ligands, wigner, trans_table, dist_index):
    tables = trans_table[dist_index]
    translated = translate(receptors, tables)
    grouping = math.gcd(ligands.shape[0], 8)
    stacked = ligands.reshape(ligands.shape[0] // grouping, grouping, ligands.shape[1], ligands.shape[2])

    def one_group(lig_group):
        return weight_sums(translated, rotate(lig_group, wigner))
    partial_sums = lax.map(one_group, stacked)
    weight_total = jnp.moveaxis(partial_sums, 0, 1).reshape(receptors.shape[0], ligands.shape[0])
    return jnp.log(weight_total)
```

```python
import functools
import math

import jax
import jax.numpy as jnp
from jax import lax
from jax.experimental import pallas as pl
from jax.experimental.pallas import tpu as pltpu
from jax.sharding import PartitionSpec as P

SLOT = 64


def packed_start(degree):
    return degree * (4 * degree * degree - 1) // 3


def degree_groups(degrees):
    left = list(range(degrees))
    groups = []
    while left:
        members = [left.pop()]
        used = 2 * members[0] + 1
        while left:
            fits = [d for d in left if used + 2 * d + 1 <= SLOT]
            if not fits:
                break
            pick = fits[-1]
            left.remove(pick)
            members.append(pick)
            used += 2 * pick + 1
        groups.append(members)
    return groups


def slot_columns(array, groups):
    parts = []
    for members in groups:
        used = 0
        for d in members:
            parts.append(array[..., d * d : d * d + 2 * d + 1])
            used += 2 * d + 1
        if used < SLOT:
            parts.append(jnp.zeros(array.shape[:-1] + (SLOT - used,), array.dtype))
    joined = jnp.concatenate(parts, axis=-1)
    return joined.reshape(array.shape[:-1] + (len(groups), SLOT))


def unpack_kernel(groups, front, w_ref, out_ref, scr):
    rows = w_ref.shape[0]
    lane = lax.broadcasted_iota(jnp.int32, (rows, 128), 1)
    for index, members in enumerate(groups):
        used = 0
        for d in members:
            extent = 2 * d + 1
            keep = (lane >= used) & (lane < used + extent)
            for m in range(extent):
                start = front + packed_start(d) + m * extent - used
                base = start // 128 * 128
                window = w_ref[:, base : base + 256].astype(jnp.float32)
                shift = start - base
                if shift:
                    window = pltpu.roll(window, 256 - shift, 1)
                scr[:, used + m, :] = jnp.where(keep, window[:, :128], 0.0)
            used += extent
        for m in range(used, SLOT):
            scr[:, m, :] = jnp.zeros((rows, 128), jnp.float32)
        out_ref[index] = scr[...].astype(jnp.bfloat16)


def unpack_wigner(wigner, groups):
    front = 128
    rows, width = wigner.shape
    total = (front + width + 127) // 128 * 128 + 256
    padded = jnp.pad(wigner, ((0, 0), (front, total - front - width)))
    qstep = 8 if rows % 16 else 16
    return pl.pallas_call(
        functools.partial(unpack_kernel, groups, front),
        grid=(rows // qstep,),
        in_specs=[pl.BlockSpec((qstep, total), lambda i: (i, 0))],
        out_specs=pl.BlockSpec((len(groups), qstep, SLOT, 128), lambda i: (0, i, 0, 0)),
        out_shape=jax.ShapeDtypeStruct((len(groups), rows, SLOT, 128), jnp.bfloat16),
        scratch_shapes=[pltpu.VMEM((qstep, SLOT, 128), jnp.float32)],
        compiler_params=pltpu.CompilerParams(vmem_limit_bytes=48 * 1024 * 1024),
        name="unpack",
    )(padded)


def score_kernel(tab_ref, rec_ref, lig_ref, wig_ref, out_ref, trans, rot, acc):
    step = pl.program_id(0)
    rad = lig_ref.shape[1]
    ligs = lig_ref.shape[2]
    rots = wig_ref.shape[1]
    dists = tab_ref.shape[1] // (2 * rad)
    recs = rec_ref.shape[2] // 128

    @pl.when(step == 0)
    def _():
        acc[...] = jnp.zeros_like(acc)

    moved = jnp.dot(tab_ref[0], rec_ref[0], preferred_element_type=jnp.float32)
    moved = moved.reshape(2, rad, dists, recs * 128)
    for xq in range(rad):
        for half in range(2):
            piece = jnp.concatenate(
                [moved[half, xq, :, r * 128 : (r + 1) * 128] for r in range(recs)], axis=0
            )
            lo = xq * 256 + half * 128
            trans[:, lo : lo + 128] = piece.astype(jnp.bfloat16)

    coeffs = lig_ref[0].reshape(rad * ligs, 256)
    lane = lax.broadcasted_iota(jnp.int32, (SLOT, 128), 1)
    zero = jnp.zeros((SLOT, 128), jnp.bfloat16)

    def one_rotation(q, carry):
        block = wig_ref[0, q]
        wide = block.astype(jnp.float32)
        other = pltpu.roll(wide, SLOT, 1).astype(jnp.bfloat16)
        pair = jnp.concatenate([block, other], axis=0)
        none = jnp.concatenate([zero, zero], axis=0)
        full = jnp.concatenate(
            [jnp.concatenate([pair, none], axis=1), jnp.concatenate([none, pair], axis=1)], axis=0
        )
        turned = jnp.dot(coeffs, full, preferred_element_type=jnp.float32).astype(jnp.bfloat16)
        row = pl.multiple_of(q * ligs, 16)
        for xq in range(rad):
            rot[pl.ds(row, ligs), xq * 256 : (xq + 1) * 256] = turned[xq * ligs : (xq + 1) * ligs]
        return carry

    lax.fori_loop(0, rots, one_rotation, 0, unroll=4)

    acc[...] += lax.dot_general(
        rot[...], trans[...], (((1,), (1,)), ((), ())), preferred_element_type=jnp.float32
    )

    @pl.when(step == pl.num_programs(0) - 1)
    def _():
        weights = jnp.exp(acc[...])
        out_ref[...] = jnp.sum(weights.reshape(rots, ligs, acc.shape[1]), axis=0)


def per_device(receptors, ligands, wigner, trans_table, dist_index):
    degrees = trans_table.shape[1]
    radial = trans_table.shape[2]
    half = radial // 2
    groups = degree_groups(degrees)
    count = len(groups)
    recs, rows, _ = receptors.shape
    props = rows // radial
    dists = dist_index.shape[0]
    nrec = lax.axis_size("rec")
    nrot = lax.axis_size("rot")
    per_col = nrec // nrot
    local_ligs = ligands.shape[0]
    ligs = local_ligs * per_col

    lig = slot_columns(ligands, groups).reshape(local_ligs, props, 2, half, count, SLOT)
    lig = jnp.transpose(lig, (4, 3, 0, 2, 1, 5)).reshape(count * half * local_ligs, 256)
    share = -(-lig.shape[0] // (16 * nrec)) * 16
    used = lig.shape[0]
    pieces = jnp.pad(lig, ((0, share * nrec - used), (0, 0))).reshape(nrec, share, 256)
    spread = lax.all_to_all(pieces, "rec", 0, 0, tiled=False)
    mine = lax.dynamic_slice_in_dim(spread, lax.axis_index("rot") * per_col, per_col, 0)
    whole = lax.all_gather(mine, "rec", axis=1, tiled=False)
    whole = whole.reshape(per_col, nrec * share, 256)[:, :used]
    whole = whole.reshape(per_col, count, half, local_ligs, 256)
    whole = jnp.moveaxis(whole, 0, 2).reshape(count, half, ligs, 256)

    turns = lax.all_gather(wigner, "rot", axis=0, tiled=True)
    rots = turns.shape[0]
    wig = unpack_wigner(turns, groups)

    most = max(len(members) for members in groups)
    depth = most * radial
    rec = slot_columns(receptors, groups).reshape(recs, props, radial, count, SLOT)
    rec = jnp.transpose(rec, (3, 2, 0, 1, 4))
    tables = jnp.transpose(trans_table[dist_index], (1, 2, 0, 3))
    owner = []
    index = []
    for members in groups:
        row = []
        for place, d in enumerate(members):
            row += [place] * (2 * d + 1)
        owner.append(row + [-1] * (SLOT - len(row)))
        index.append(list(members) + [members[-1]] * (most - len(members)))
    owner = jnp.array(owner, jnp.int32)
    keep = owner[:, None, :] == jnp.arange(most, dtype=jnp.int32)[None, :, None]
    rec = jnp.where(keep[:, :, None, None, None, :], rec[:, None], jnp.zeros((), rec.dtype))
    rec = rec.reshape(count, depth, recs * props * SLOT)
    tab = jnp.stack(
        [jnp.concatenate([tables[d] for d in row], axis=-1) for row in index]
    ).reshape(count, radial * dists, depth)

    sums = pl.pallas_call(
        score_kernel,
        grid=(count,),
        in_specs=[
            pl.BlockSpec((1, radial * dists, depth), lambda i: (i, 0, 0)),
            pl.BlockSpec((1, depth, recs * 128), lambda i: (i, 0, 0)),
            pl.BlockSpec((1, half, ligs, 256), lambda i: (i, 0, 0, 0)),
            pl.BlockSpec((1, rots, SLOT, 128), lambda i: (i, 0, 0, 0)),
        ],
        out_specs=pl.BlockSpec((ligs, recs * dists), lambda i: (0, 0)),
        out_shape=jax.ShapeDtypeStruct((ligs, recs * dists), jnp.float32),
        scratch_shapes=[
            pltpu.VMEM((recs * dists, half * 256), jnp.bfloat16),
            pltpu.VMEM((rots * ligs, half * 256), jnp.bfloat16),
            pltpu.VMEM((rots * ligs, recs * dists), jnp.float32),
        ],
        compiler_params=pltpu.CompilerParams(vmem_limit_bytes=48 * 1024 * 1024),
        name="scores",
    )(tab, rec, whole, wig)
    totals = jnp.sum(sums.reshape(ligs, recs, dists), axis=2)
    return jnp.log(totals.T)


def solution(mesh):
    in_specs = (P("rec", None, None), P("rec", None, None), P("rot", None), P(), P())
    out_specs = P("rec", "rot")
    return jax.shard_map(
        per_device, mesh=mesh, in_specs=in_specs, out_specs=out_specs, check_vma=False
    )
```

```python
import functools
import math

import jax
import jax.numpy as jnp
from jax import lax
from jax.experimental import pallas as pl
from jax.experimental.pallas import tpu as pltpu
from jax.sharding import PartitionSpec as P

SLOT = 64


def packed_start(degree):
    return degree * (4 * degree * degree - 1) // 3


def degree_groups(degrees):
    left = list(range(degrees))
    groups = []
    while left:
        members = [left.pop()]
        used = 2 * members[0] + 1
        while left:
            fits = [d for d in left if used + 2 * d + 1 <= SLOT]
            if not fits:
                break
            pick = fits[-1]
            left.remove(pick)
            members.append(pick)
            used += 2 * pick + 1
        groups.append(members)
    return groups


def column_sources(groups):
    sources = []
    for members in groups + [[]] * (len(groups) % 2):
        row = []
        for d in members:
            row += range(d * d, d * d + 2 * d + 1)
        sources += row + [-1] * (SLOT - len(row))
    return jnp.array(sources, jnp.int32)[None, :]


def select_columns(source, rows):
    shape = (rows.shape[-1], source.shape[1])
    hit = lax.broadcasted_iota(jnp.int32, shape, 0) == source
    return jnp.dot(
        rows, jnp.where(hit, 1.0, 0.0).astype(jnp.bfloat16), preferred_element_type=jnp.float32
    )


def merge_slots(first, second, group):
    lo = group // 2 * 128
    first = first[:, lo : lo + 128]
    second = second[:, lo : lo + 128]
    lane = lax.broadcasted_iota(jnp.int32, first.shape, 1)
    if group % 2:
        return jnp.where(lane < SLOT, pltpu.roll(first, SLOT, 1), second)
    return jnp.where(lane < SLOT, first, pltpu.roll(second, SLOT, 1))


def ligand_kernel(source_ref, lig_ref, out_ref):
    count, rows, _ = out_ref.shape
    slots = select_columns(source_ref[...], lig_ref[...])
    for group in range(count):
        for half in range(2):
            first = slots[half * 2 * rows : (half * 2 + 1) * rows]
            second = slots[(half * 2 + 1) * rows : (half * 2 + 2) * rows]
            merged = merge_slots(first, second, group)
            out_ref[group, :, half * 128 : (half + 1) * 128] = merged.astype(jnp.bfloat16)


def receptor_kernel(groups, depth, source_ref, rec_ref, out_ref):
    slots = select_columns(source_ref[...], rec_ref[...])
    recs = out_ref.shape[2] // 128
    lane = lax.broadcasted_iota(jnp.int32, (depth, 128), 1) % SLOT
    for group, members in enumerate(groups):
        split = 2 * members[0] + 1
        for r in range(recs):
            first = slots[2 * r * depth : (2 * r + 1) * depth]
            second = slots[(2 * r + 1) * depth : (2 * r + 2) * depth]
            merged = merge_slots(first, second, group)
            both = jnp.concatenate(
                [jnp.where(lane < split, merged, 0.0), jnp.where(lane < split, 0.0, merged)], axis=0
            )
            out_ref[group, :, r * 128 : (r + 1) * 128] = both.astype(jnp.bfloat16)


def unpack_kernel(groups, front, w_ref, out_ref, scr):
    rows = w_ref.shape[0]
    lane = lax.broadcasted_iota(jnp.int32, (rows, 128), 1)
    for index, members in enumerate(groups):
        used = 0
        for d in members:
            extent = 2 * d + 1
            keep = (lane >= used) & (lane < used + extent)
            for m in range(extent):
                start = front + packed_start(d) + m * extent - used
                base = start // 128 * 128
                window = w_ref[:, base : base + 256].astype(jnp.float32)
                shift = start - base
                if shift:
                    window = pltpu.roll(window, 256 - shift, 1)
                scr[:, used + m, :] = jnp.where(keep, window[:, :128], 0.0)
            used += extent
        for m in range(used, SLOT):
            scr[:, m, :] = jnp.zeros((rows, 128), jnp.float32)
        out_ref[index] = scr[...].astype(jnp.bfloat16)


def unpack_wigner(wigner, groups):
    front = 128
    rows, width = wigner.shape
    total = (front + width + 127) // 128 * 128 + 256
    padded = jnp.pad(wigner, ((0, 0), (front, total - front - width)))
    qstep = 8 if rows % 16 else 16
    return pl.pallas_call(
        functools.partial(unpack_kernel, groups, front),
        grid=(rows // qstep,),
        in_specs=[pl.BlockSpec((qstep, total), lambda i: (i, 0))],
        out_specs=pl.BlockSpec((len(groups), qstep, SLOT, 128), lambda i: (0, i, 0, 0)),
        out_shape=jax.ShapeDtypeStruct((len(groups), rows, SLOT, 128), jnp.bfloat16),
        scratch_shapes=[pltpu.VMEM((qstep, SLOT, 128), jnp.float32)],
        compiler_params=pltpu.CompilerParams(vmem_limit_bytes=48 * 1024 * 1024),
        name="unpack",
    )(padded)


def score_kernel(
    tab_ref, rec_ref, lig_a_ref, lig_b_ref, wig_a_ref, wig_b_ref, out_ref, trans, rot, acc
):
    step = pl.program_id(0)
    rots = wig_a_ref.shape[1]
    recs = rec_ref.shape[2] // 128
    rad = trans.shape[1] // 256
    dists = tab_ref.shape[1] // (2 * rad)
    part = lig_a_ref.shape[1] // rad
    ligs = 2 * part

    @pl.when(step == 0)
    def _():
        acc[...] = jnp.zeros_like(acc)

    moved = jnp.dot(tab_ref[0], rec_ref[0], preferred_element_type=jnp.float32)
    moved = moved.reshape(2, rad, dists, recs * 128)
    for xq in range(rad):
        for half in range(2):
            piece = jnp.concatenate(
                [moved[half, xq, :, r * 128 : (r + 1) * 128] for r in range(recs)], axis=0
            )
            lo = xq * 256 + half * 128
            trans[:, lo : lo + 128] = piece.astype(jnp.bfloat16)

    low = lig_a_ref[0].astype(jnp.float32)
    high = lig_b_ref[0].astype(jnp.float32)
    rows = []
    for xq in range(rad):
        rows.append(low[xq * part : (xq + 1) * part])
        rows.append(high[xq * part : (xq + 1) * part])
    coeffs = jnp.concatenate(rows, axis=0).astype(jnp.bfloat16)
    none = jnp.zeros((2 * SLOT, 128), jnp.bfloat16)

    for source, wig_ref in enumerate((wig_a_ref, wig_b_ref)):

        def one_rotation(q, carry, wig_ref=wig_ref, source=source):
            block = wig_ref[0, q]
            other = pltpu.roll(block.astype(jnp.float32), SLOT, 1).astype(jnp.bfloat16)
            pair = jnp.concatenate([block, other], axis=0)
            full = jnp.concatenate(
                [jnp.concatenate([pair, none], axis=1), jnp.concatenate([none, pair], axis=1)],
                axis=0,
            )
            turned = jnp.dot(coeffs, full, preferred_element_type=jnp.float32).astype(jnp.bfloat16)
            row = pl.multiple_of((q + source * rots) * ligs, 16)
            for xq in range(rad):
                rot[pl.ds(row, ligs), xq * 256 : (xq + 1) * 256] = turned[
                    xq * ligs : (xq + 1) * ligs
                ]
            return carry

        lax.fori_loop(0, rots, one_rotation, 0, unroll=4)

    acc[...] += lax.dot_general(
        rot[...], trans[...], (((1,), (1,)), ((), ())), preferred_element_type=jnp.float32
    )

    @pl.when(step == pl.num_programs(0) - 1)
    def _():
        weights = jnp.exp(acc[...])
        out_ref[...] = jnp.sum(weights.reshape(2 * rots, ligs, acc.shape[1]), axis=0)


def per_device(receptors, ligands, wigner, trans_table, dist_index):
    degrees = trans_table.shape[1]
    radial = trans_table.shape[2]
    half = radial // 2
    groups = degree_groups(degrees)
    count = len(groups)
    padded = count + count % 2
    source = column_sources(groups)
    recs, rows, angular = receptors.shape
    props = rows // radial
    dists = dist_index.shape[0]
    nrec = lax.axis_size("rec")
    part = ligands.shape[0]
    ligs = 2 * part
    params = pltpu.CompilerParams(vmem_limit_bytes=48 * 1024 * 1024)
    core = lax.axis_index("rec") % 2
    swap = [(i, i ^ 1) for i in range(nrec)]
    same_core = [list(range(c, nrec, 2)) for c in range(2)]

    share = wigner.shape[0] // 2
    own = lax.dynamic_slice_in_dim(wigner, core * share, share, 0)
    turns_a = lax.all_gather(own, "rot", axis=0, tiled=True)
    turns_b = lax.ppermute(turns_a, "rec", swap)
    rots = turns_a.shape[0]

    lig = ligands.reshape(part, props, 2, half, angular)
    lig = jnp.transpose(lig, (2, 1, 3, 0, 4)).reshape(4 * half * part, angular)
    lig = pl.pallas_call(
        ligand_kernel,
        out_shape=jax.ShapeDtypeStruct((padded, half * part, 256), jnp.bfloat16),
        compiler_params=params,
        name="ligand_slots",
    )(source, lig)
    pieces = lig.reshape(nrec // 2, -1, 256)
    spread = lax.all_to_all(pieces, "rec", 0, 0, axis_index_groups=same_core)
    mine = lax.dynamic_index_in_dim(spread, lax.axis_index("rot"), 0, keepdims=False)
    lig_a = lax.all_gather(mine, "rec", axis=0, axis_index_groups=same_core)
    lig_b = lax.ppermute(lig_a, "rec", swap)
    lig_a = lig_a.reshape(padded, half * part, 256)
    lig_b = lig_b.reshape(padded, half * part, 256)

    wig_a = unpack_wigner(turns_a, groups)
    wig_b = unpack_wigner(turns_b, groups)

    deep = (radial + 15) // 16 * 16
    rec = receptors.reshape(recs * props, radial, angular)
    rec = jnp.pad(rec, ((0, 0), (0, deep - radial), (0, 0))).reshape(-1, angular)
    rec = pl.pallas_call(
        functools.partial(receptor_kernel, groups, deep),
        out_shape=jax.ShapeDtypeStruct((count, 2 * deep, recs * 128), jnp.bfloat16),
        compiler_params=params,
        name="receptor_slots",
    )(source, rec)
    tables = jnp.transpose(trans_table[dist_index], (1, 2, 0, 3))
    tables = jnp.pad(tables, ((0, 0), (0, 0), (0, 0), (0, deep - radial)))
    tab = jnp.stack([jnp.concatenate([tables[d] for d in row], axis=-1) for row in groups])
    tab = tab.reshape(count, radial * dists, 2 * deep)

    sums = pl.pallas_call(
        score_kernel,
        grid=(count,),
        in_specs=[
            pl.BlockSpec((1, radial * dists, 2 * deep), lambda i: (i, 0, 0)),
            pl.BlockSpec((1, 2 * deep, recs * 128), lambda i: (i, 0, 0)),
            pl.BlockSpec((1, half * part, 256), lambda i: (i, 0, 0)),
            pl.BlockSpec((1, half * part, 256), lambda i: (i, 0, 0)),
            pl.BlockSpec((1, rots, SLOT, 128), lambda i: (i, 0, 0, 0)),
            pl.BlockSpec((1, rots, SLOT, 128), lambda i: (i, 0, 0, 0)),
        ],
        out_specs=pl.BlockSpec((ligs, recs * dists), lambda i: (0, 0)),
        out_shape=jax.ShapeDtypeStruct((ligs, recs * dists), jnp.float32),
        scratch_shapes=[
            pltpu.VMEM((recs * dists, half * 256), jnp.bfloat16),
            pltpu.VMEM((2 * rots * ligs, half * 256), jnp.bfloat16),
            pltpu.VMEM((2 * rots * ligs, recs * dists), jnp.float32),
        ],
        compiler_params=params,
        name="scores",
    )(tab, rec, lig_a, lig_b, wig_a, wig_b)
    totals = jnp.sum(sums.reshape(2, part, recs, dists), axis=3)
    totals = jnp.where(core == 0, totals, totals[::-1]).reshape(ligs, recs)
    return jnp.log(totals.T)


def solution(mesh):
    in_specs = (P("rec", None, None), P("rec", None, None), P("rot", None), P(), P())
    out_specs = P("rec", "rot")
    return jax.shard_map(
        per_device, mesh=mesh, in_specs=in_specs, out_specs=out_specs, check_vma=False
    )
```

```python
import functools
import math

import jax
import jax.numpy as jnp
from jax import lax
from jax.experimental import pallas as pl
from jax.experimental.pallas import tpu as pltpu
from jax.sharding import PartitionSpec as P

SLOT = 64


def packed_start(degree):
    return degree * (4 * degree * degree - 1) // 3


def degree_groups(degrees):
    left = list(range(degrees))
    groups = []
    while left:
        members = [left.pop()]
        used = 2 * members[0] + 1
        while left:
            fits = [d for d in left if used + 2 * d + 1 <= SLOT]
            if not fits:
                break
            pick = fits[-1]
            left.remove(pick)
            members.append(pick)
            used += 2 * pick + 1
        groups.append(members)
    return groups


def column_sources(groups):
    sources = []
    for members in groups + [[]] * (len(groups) % 2):
        row = []
        for d in members:
            row += range(d * d, d * d + 2 * d + 1)
        sources += row + [-1] * (SLOT - len(row))
    return jnp.array(sources, jnp.int32)[None, :]


def select_columns(source, rows):
    shape = (rows.shape[-1], source.shape[1])
    hit = lax.broadcasted_iota(jnp.int32, shape, 0) == source
    return jnp.dot(
        rows, jnp.where(hit, 1.0, 0.0).astype(jnp.bfloat16), preferred_element_type=jnp.float32
    )


def merge_slots(first, second, group):
    lo = group // 2 * 128
    first = first[:, lo : lo + 128]
    second = second[:, lo : lo + 128]
    lane = lax.broadcasted_iota(jnp.int32, first.shape, 1)
    if group % 2:
        return jnp.where(lane < SLOT, pltpu.roll(first, SLOT, 1), second)
    return jnp.where(lane < SLOT, first, pltpu.roll(second, SLOT, 1))


def ligand_kernel(source_ref, lig_ref, out_ref):
    count, rows, _ = out_ref.shape
    slots = select_columns(source_ref[...], lig_ref[...])
    for group in range(count):
        for half in range(2):
            first = slots[half * 2 * rows : (half * 2 + 1) * rows]
            second = slots[(half * 2 + 1) * rows : (half * 2 + 2) * rows]
            merged = merge_slots(first, second, group)
            out_ref[group, :, half * 128 : (half + 1) * 128] = merged.astype(jnp.bfloat16)


def receptor_kernel(groups, depth, source_ref, rec_ref, out_ref):
    slots = select_columns(source_ref[...], rec_ref[...])
    recs = out_ref.shape[2] // 128
    lane = lax.broadcasted_iota(jnp.int32, (depth, 128), 1) % SLOT
    for group, members in enumerate(groups):
        split = 2 * members[0] + 1
        for r in range(recs):
            first = slots[2 * r * depth : (2 * r + 1) * depth]
            second = slots[(2 * r + 1) * depth : (2 * r + 2) * depth]
            merged = merge_slots(first, second, group)
            both = jnp.concatenate(
                [jnp.where(lane < split, merged, 0.0), jnp.where(lane < split, 0.0, merged)], axis=0
            )
            out_ref[group, :, r * 128 : (r + 1) * 128] = both.astype(jnp.bfloat16)


def unpack_kernel(groups, front, w_ref, out_ref, scr):
    rows = w_ref.shape[0]
    lane = lax.broadcasted_iota(jnp.int32, (rows, 128), 1)
    for index, members in enumerate(groups):
        used = 0
        for d in members:
            extent = 2 * d + 1
            keep = (lane >= used) & (lane < used + extent)
            for m in range(extent):
                start = front + packed_start(d) + m * extent - used
                base = start // 128 * 128
                window = w_ref[:, base : base + 256].astype(jnp.float32)
                shift = start - base
                if shift:
                    window = pltpu.roll(window, 256 - shift, 1)
                scr[:, used + m, :] = jnp.where(keep, window[:, :128], 0.0)
            used += extent
        for m in range(used, SLOT):
            scr[:, m, :] = jnp.zeros((rows, 128), jnp.float32)
        out_ref[index] = scr[...].astype(jnp.bfloat16)


def unpack_wigner(wigner, groups):
    front = 128
    rows, width = wigner.shape
    total = (front + width + 127) // 128 * 128 + 256
    padded = jnp.pad(wigner, ((0, 0), (front, total - front - width)))
    qstep = 8 if rows % 16 else 16
    return pl.pallas_call(
        functools.partial(unpack_kernel, groups, front),
        grid=(rows // qstep,),
        in_specs=[pl.BlockSpec((qstep, total), lambda i: (i, 0))],
        out_specs=pl.BlockSpec((len(groups), qstep, SLOT, 128), lambda i: (0, i, 0, 0)),
        out_shape=jax.ShapeDtypeStruct((len(groups), rows, SLOT, 128), jnp.bfloat16),
        scratch_shapes=[pltpu.VMEM((qstep, SLOT, 128), jnp.float32)],
        compiler_params=pltpu.CompilerParams(vmem_limit_bytes=48 * 1024 * 1024),
        name="unpack",
    )(padded)


def score_kernel(
    where_ref, tab_ref, rec_ref, lig_a_ref, lig_b_ref, wig_a_ref, wig_b_ref, out_ref, trans, rot, acc
):
    step = pl.program_id(0)
    rots = wig_a_ref.shape[1]
    recs = rec_ref.shape[2] // 128
    rad = trans.shape[1] // 256
    dists = tab_ref.shape[1] // (2 * rad)
    part = lig_a_ref.shape[1] // rad
    ligs = 2 * part

    @pl.when(step == 0)
    def _():
        acc[...] = jnp.zeros_like(acc)

    moved = jnp.dot(tab_ref[0], rec_ref[0], preferred_element_type=jnp.float32)
    moved = moved.reshape(2, rad, dists, recs * 128)
    for xq in range(rad):
        for half in range(2):
            piece = jnp.concatenate(
                [moved[half, xq, :, r * 128 : (r + 1) * 128] for r in range(recs)], axis=0
            )
            lo = xq * 256 + half * 128
            trans[:, lo : lo + 128] = piece.astype(jnp.bfloat16)

    low = lig_a_ref[0].astype(jnp.float32)
    high = lig_b_ref[0].astype(jnp.float32)
    rows = []
    for xq in range(rad):
        rows.append(low[xq * part : (xq + 1) * part])
        rows.append(high[xq * part : (xq + 1) * part])
    coeffs = jnp.concatenate(rows, axis=0).astype(jnp.bfloat16)
    none = jnp.zeros((2 * SLOT, 128), jnp.bfloat16)

    for source, wig_ref in enumerate((wig_a_ref, wig_b_ref)):

        def one_rotation(q, carry, wig_ref=wig_ref, source=source):
            block = wig_ref[0, q]
            other = pltpu.roll(block.astype(jnp.float32), SLOT, 1).astype(jnp.bfloat16)
            pair = jnp.concatenate([block, other], axis=0)
            full = jnp.concatenate(
                [jnp.concatenate([pair, none], axis=1), jnp.concatenate([none, pair], axis=1)],
                axis=0,
            )
            turned = jnp.dot(coeffs, full, preferred_element_type=jnp.float32).astype(jnp.bfloat16)
            row = pl.multiple_of((q + source * rots) * ligs, 16)
            for xq in range(rad):
                rot[pl.ds(row, ligs), xq * 256 : (xq + 1) * 256] = turned[
                    xq * ligs : (xq + 1) * ligs
                ]
            return carry

        lax.fori_loop(0, rots, one_rotation, 0, unroll=True)

    acc[...] += lax.dot_general(
        rot[...], trans[...], (((1,), (1,)), ((), ())), preferred_element_type=jnp.float32
    )

    @pl.when(step == pl.num_programs(0) - 1)
    def _():
        weights = jnp.exp(acc[...])
        out_ref[...] = jnp.sum(weights.reshape(2 * rots, ligs, acc.shape[1]), axis=0)


def per_device(receptors, ligands, wigner, trans_table, dist_index):
    degrees = trans_table.shape[1]
    radial = trans_table.shape[2]
    half = radial // 2
    groups = degree_groups(degrees)
    count = len(groups)
    padded = count + count % 2
    source = column_sources(groups)
    recs, rows, angular = receptors.shape
    props = rows // radial
    dists = dist_index.shape[0]
    nrec = lax.axis_size("rec")
    part = ligands.shape[0]
    ligs = 2 * part
    params = pltpu.CompilerParams(vmem_limit_bytes=48 * 1024 * 1024)
    core = lax.axis_index("rec") % 2
    swap = [(i, i ^ 1) for i in range(nrec)]
    same_core = [list(range(c, nrec, 2)) for c in range(2)]

    share = wigner.shape[0] // 2
    own = lax.dynamic_slice_in_dim(wigner, core * share, share, 0)
    turns_a = lax.all_gather(own, "rot", axis=0, tiled=True)
    turns_b = lax.ppermute(turns_a, "rec", swap)
    rots = turns_a.shape[0]

    lig = ligands.reshape(part, props, 2, half, angular)
    lig = jnp.transpose(lig, (2, 1, 3, 0, 4)).reshape(4 * half * part, angular)
    lig = pl.pallas_call(
        ligand_kernel,
        out_shape=jax.ShapeDtypeStruct((padded, half * part, 256), jnp.bfloat16),
        compiler_params=params,
        name="ligand_slots",
    )(source, lig)
    pieces = lig.reshape(nrec // 2, -1, 256)
    spread = lax.all_to_all(pieces, "rec", 0, 0, axis_index_groups=same_core)
    mine = lax.dynamic_index_in_dim(spread, lax.axis_index("rot"), 0, keepdims=False)
    found = [mine]
    for k in range(1, nrec // 2):
        found.append(lax.ppermute(mine, "rec", [(i, i ^ (2 * k)) for i in range(nrec)]))
    lig_a = jnp.concatenate(found, axis=0).reshape(padded, half * part, 256)
    lig_b = lax.ppermute(lig_a, "rec", swap)
    each = padded // (nrec // 2)
    order = jnp.arange(count, dtype=jnp.int32)
    chip = (lax.axis_index("rec") // 2).astype(jnp.int32)
    where = (chip ^ (order // each)) * each + order % each

    wig_a = unpack_wigner(turns_a, groups)
    wig_b = unpack_wigner(turns_b, groups)

    deep = (radial + 15) // 16 * 16
    rec = receptors.reshape(recs * props, radial, angular)
    rec = jnp.pad(rec, ((0, 0), (0, deep - radial), (0, 0))).reshape(-1, angular)
    rec = pl.pallas_call(
        functools.partial(receptor_kernel, groups, deep),
        out_shape=jax.ShapeDtypeStruct((count, 2 * deep, recs * 128), jnp.bfloat16),
        compiler_params=params,
        name="receptor_slots",
    )(source, rec)
    tables = jnp.transpose(trans_table[dist_index], (1, 2, 0, 3))
    tables = jnp.pad(tables, ((0, 0), (0, 0), (0, 0), (0, deep - radial)))
    tab = jnp.stack([jnp.concatenate([tables[d] for d in row], axis=-1) for row in groups])
    tab = tab.reshape(count, radial * dists, 2 * deep)

    sums = pl.pallas_call(
        score_kernel,
        grid_spec=pltpu.PrefetchScalarGridSpec(
            num_scalar_prefetch=1,
            grid=(count,),
            in_specs=[
                pl.BlockSpec((1, radial * dists, 2 * deep), lambda i, w: (i, 0, 0)),
                pl.BlockSpec((1, 2 * deep, recs * 128), lambda i, w: (i, 0, 0)),
                pl.BlockSpec((1, half * part, 256), lambda i, w: (w[i], 0, 0)),
                pl.BlockSpec((1, half * part, 256), lambda i, w: (w[i], 0, 0)),
                pl.BlockSpec((1, rots, SLOT, 128), lambda i, w: (i, 0, 0, 0)),
                pl.BlockSpec((1, rots, SLOT, 128), lambda i, w: (i, 0, 0, 0)),
            ],
            out_specs=pl.BlockSpec((ligs, recs * dists), lambda i, w: (0, 0)),
            scratch_shapes=[
                pltpu.VMEM((recs * dists, half * 256), jnp.bfloat16),
                pltpu.VMEM((2 * rots * ligs, half * 256), jnp.bfloat16),
                pltpu.VMEM((2 * rots * ligs, recs * dists), jnp.float32),
            ],
        ),
        out_shape=jax.ShapeDtypeStruct((ligs, recs * dists), jnp.float32),
        compiler_params=params,
        name="scores",
    )(where, tab, rec, lig_a, lig_b, wig_a, wig_b)
    totals = jnp.sum(sums.reshape(2, part, recs, dists), axis=3)
    totals = jnp.where(core == 0, totals, totals[::-1]).reshape(ligs, recs)
    return jnp.log(totals.T)


def solution(mesh):
    in_specs = (P("rec", None, None), P("rec", None, None), P("rot", None), P(), P())
    out_specs = P("rec", "rot")
    return jax.shard_map(
        per_device, mesh=mesh, in_specs=in_specs, out_specs=out_specs, check_vma=False
    )
```

```python
import functools
import math

import jax
import jax.numpy as jnp
from jax import lax
from jax.experimental import pallas as pl
from jax.experimental.pallas import tpu as pltpu
from jax.sharding import PartitionSpec as P

SLOT = 64


def packed_start(degree):
    return degree * (4 * degree * degree - 1) // 3


def degree_groups(degrees):
    left = list(range(degrees))
    groups = []
    while left:
        members = [left.pop()]
        used = 2 * members[0] + 1
        while left:
            fits = [d for d in left if used + 2 * d + 1 <= SLOT]
            if not fits:
                break
            pick = fits[-1]
            left.remove(pick)
            members.append(pick)
            used += 2 * pick + 1
        groups.append(members)
    return groups


def column_sources(groups):
    sources = []
    for members in groups + [[]] * (len(groups) % 2):
        row = []
        for d in members:
            row += range(d * d, d * d + 2 * d + 1)
        sources += row + [-1] * (SLOT - len(row))
    return jnp.array(sources, jnp.int32)[None, :]


def select_columns(source, rows):
    shape = (rows.shape[-1], source.shape[1])
    hit = lax.broadcasted_iota(jnp.int32, shape, 0) == source
    return jnp.dot(
        rows, jnp.where(hit, 1.0, 0.0).astype(jnp.bfloat16), preferred_element_type=jnp.float32
    )


def merge_slots(first, second, group):
    lo = group // 2 * 128
    first = first[:, lo : lo + 128]
    second = second[:, lo : lo + 128]
    lane = lax.broadcasted_iota(jnp.int32, first.shape, 1)
    if group % 2:
        return jnp.where(lane < SLOT, pltpu.roll(first, SLOT, 1), second)
    return jnp.where(lane < SLOT, first, pltpu.roll(second, SLOT, 1))


def ligand_kernel(source_ref, lig_ref, out_ref):
    count, rows, _ = out_ref.shape
    slots = select_columns(source_ref[...], lig_ref[...])
    for group in range(count):
        for half in range(2):
            first = slots[half * 2 * rows : (half * 2 + 1) * rows]
            second = slots[(half * 2 + 1) * rows : (half * 2 + 2) * rows]
            merged = merge_slots(first, second, group)
            out_ref[group, :, half * 128 : (half + 1) * 128] = merged.astype(jnp.bfloat16)


def receptor_kernel(groups, depth, source_ref, rec_ref, out_ref):
    slots = select_columns(source_ref[...], rec_ref[...])
    recs = out_ref.shape[2] // 128
    lane = lax.broadcasted_iota(jnp.int32, (depth, 128), 1) % SLOT
    for group, members in enumerate(groups):
        split = 2 * members[0] + 1
        for r in range(recs):
            first = slots[2 * r * depth : (2 * r + 1) * depth]
            second = slots[(2 * r + 1) * depth : (2 * r + 2) * depth]
            merged = merge_slots(first, second, group)
            both = jnp.concatenate(
                [jnp.where(lane < split, merged, 0.0), jnp.where(lane < split, 0.0, merged)], axis=0
            )
            out_ref[group, :, r * 128 : (r + 1) * 128] = both.astype(jnp.bfloat16)


def unpack_kernel(groups, w_ref, out_ref, flat, scr):
    blocks, share, width = w_ref.shape
    rows = blocks * share
    for part in range(blocks):
        flat[part * share : (part + 1) * share, :width] = w_ref[part].astype(jnp.float32)
    lane = lax.broadcasted_iota(jnp.int32, (rows, 128), 1)
    for index, members in enumerate(groups):
        used = 0
        for d in members:
            extent = 2 * d + 1
            keep = (lane >= used) & (lane < used + extent)
            for m in range(extent):
                start = packed_start(d) + m * extent
                base = start // 128 * 128
                shift = (used - start) % 128
                window = flat[:, base : base + 128]
                if shift:
                    window = pltpu.roll(window, shift, 1)
                first = base + 128 - start
                if first < extent:
                    rest = flat[:, base + 128 : base + 256]
                    if shift:
                        rest = pltpu.roll(rest, shift, 1)
                    window = jnp.where(lane < used + first, window, rest)
                scr[:, used + m, :] = jnp.where(keep, window, 0.0)
            used += extent
        for m in range(used, SLOT):
            scr[:, m, :] = jnp.zeros((rows, 128), jnp.float32)
        out_ref[index] = scr[...].astype(jnp.bfloat16)


def unpack_wigner(wigner, groups):
    parts, share, width = wigner.shape
    rows = parts * share
    blocks = math.gcd(parts, max(16 // share, 1))
    qstep = blocks * share
    total = (width + 127) // 128 * 128 + 128
    return pl.pallas_call(
        functools.partial(unpack_kernel, groups),
        grid=(parts // blocks,),
        in_specs=[pl.BlockSpec((blocks, share, width), lambda i: (i, 0, 0))],
        out_specs=pl.BlockSpec((len(groups), qstep, SLOT, 128), lambda i: (0, i, 0, 0)),
        out_shape=jax.ShapeDtypeStruct((len(groups), rows, SLOT, 128), jnp.bfloat16),
        scratch_shapes=[
            pltpu.VMEM((qstep, total), jnp.float32),
            pltpu.VMEM((qstep, SLOT, 128), jnp.float32),
        ],
        compiler_params=pltpu.CompilerParams(vmem_limit_bytes=48 * 1024 * 1024),
        name="unpack",
    )(wigner)


def score_kernel(
    where_ref,
    one_ref,
    two_ref,
    tab_a_ref,
    tab_b_ref,
    rec_ref,
    lig_a_ref,
    lig_b_ref,
    wig_a_ref,
    wig_b_ref,
    out_ref,
    table,
    trans,
    rot,
    acc,
):
    step = pl.program_id(0)
    rots = wig_a_ref.shape[1]
    recs = rec_ref.shape[2] // 128
    rad = trans.shape[1] // 256
    dists = tab_a_ref.shape[1] // (2 * rad)
    radial = tab_a_ref.shape[2]
    part = lig_a_ref.shape[1] // rad
    ligs = 2 * part

    @pl.when(step == 0)
    def _():
        acc[...] = jnp.zeros_like(acc)
        table[...] = jnp.zeros_like(table)

    deep = table.shape[1] // 2
    table[:, :radial] = tab_a_ref[0]
    table[:, deep : deep + radial] = tab_b_ref[0]
    moved = jnp.dot(table[...], rec_ref[0], preferred_element_type=jnp.float32)
    moved = moved.reshape(2, rad, dists, recs * 128)
    for xq in range(rad):
        for half in range(2):
            piece = jnp.concatenate(
                [moved[half, xq, :, r * 128 : (r + 1) * 128] for r in range(recs)], axis=0
            )
            lo = xq * 256 + half * 128
            trans[:, lo : lo + 128] = piece.astype(jnp.bfloat16)

    low = lig_a_ref[0].astype(jnp.float32)
    high = lig_b_ref[0].astype(jnp.float32)
    rows = []
    for xq in range(rad):
        rows.append(low[xq * part : (xq + 1) * part])
        rows.append(high[xq * part : (xq + 1) * part])
    coeffs = jnp.concatenate(rows, axis=0).astype(jnp.bfloat16)
    none = jnp.zeros((2 * SLOT, 128), jnp.bfloat16)

    for source, wig_ref in enumerate((wig_a_ref, wig_b_ref)):

        def one_rotation(q, carry, wig_ref=wig_ref, source=source):
            block = wig_ref[0, q]
            other = pltpu.roll(block.astype(jnp.float32), SLOT, 1).astype(jnp.bfloat16)
            pair = jnp.concatenate([block, other], axis=0)
            full = jnp.concatenate(
                [jnp.concatenate([pair, none], axis=1), jnp.concatenate([none, pair], axis=1)],
                axis=0,
            )
            turned = jnp.dot(coeffs, full, preferred_element_type=jnp.float32).astype(jnp.bfloat16)
            row = pl.multiple_of((q + source * rots) * ligs, 16)
            for xq in range(rad):
                rot[pl.ds(row, ligs), xq * 256 : (xq + 1) * 256] = turned[
                    xq * ligs : (xq + 1) * ligs
                ]
            return carry

        lax.fori_loop(0, rots, one_rotation, 0, unroll=True)

    acc[...] += lax.dot_general(
        rot[...], trans[...], (((1,), (1,)), ((), ())), preferred_element_type=jnp.float32
    )

    @pl.when(step == pl.num_programs(0) - 1)
    def _():
        weights = jnp.exp(acc[...])
        out_ref[...] = jnp.sum(weights.reshape(2 * rots, ligs, acc.shape[1]), axis=0)


def per_device(receptors, ligands, wigner, trans_table, dist_index):
    degrees = trans_table.shape[1]
    radial = trans_table.shape[2]
    half = radial // 2
    groups = degree_groups(degrees)
    count = len(groups)
    padded = count + count % 2
    source = column_sources(groups)
    recs, rows, angular = receptors.shape
    props = rows // radial
    dists = dist_index.shape[0]
    nrec = lax.axis_size("rec")
    part = ligands.shape[0]
    ligs = 2 * part
    params = pltpu.CompilerParams(vmem_limit_bytes=48 * 1024 * 1024)
    core = lax.axis_index("rec") % 2
    swap = [(i, i ^ 1) for i in range(nrec)]
    same_core = [list(range(c, nrec, 2)) for c in range(2)]

    share = wigner.shape[0] // 2
    own = lax.dynamic_slice_in_dim(wigner, core * share, share, 0)
    turns_a = lax.all_gather(own, "rot", axis=0)
    turns_b = lax.ppermute(turns_a, "rec", swap)
    rots = turns_a.shape[0] * share

    lig = ligands.reshape(part, props, 2, half, angular)
    lig = jnp.transpose(lig, (2, 1, 3, 0, 4)).reshape(4 * half * part, angular)
    lig = pl.pallas_call(
        ligand_kernel,
        out_shape=jax.ShapeDtypeStruct((padded, half * part, 256), jnp.bfloat16),
        compiler_params=params,
        name="ligand_slots",
    )(source, lig)
    pieces = lig.reshape(nrec // 2, -1, 256)
    spread = lax.all_to_all(pieces, "rec", 0, 0, axis_index_groups=same_core)
    mine = lax.dynamic_index_in_dim(spread, lax.axis_index("rot"), 0, keepdims=False)
    found = [mine]
    for k in range(1, nrec // 2):
        found.append(lax.ppermute(mine, "rec", [(i, i ^ (2 * k)) for i in range(nrec)]))
    lig_a = jnp.concatenate(found, axis=0).reshape(padded, half * part, 256)
    lig_b = lax.ppermute(lig_a, "rec", swap)
    each = padded // (nrec // 2)
    order = jnp.arange(count, dtype=jnp.int32)
    chip = (lax.axis_index("rec") // 2).astype(jnp.int32)
    where = (chip ^ (order // each)) * each + order % each

    wig_a = unpack_wigner(turns_a, groups)
    wig_b = unpack_wigner(turns_b, groups)

    deep = (radial + 15) // 16 * 16
    rec = receptors.reshape(recs * props, radial, angular)
    rec = jnp.pad(rec, ((0, 0), (0, deep - radial), (0, 0))).reshape(-1, angular)
    rec = pl.pallas_call(
        functools.partial(receptor_kernel, groups, deep),
        out_shape=jax.ShapeDtypeStruct((count, 2 * deep, recs * 128), jnp.bfloat16),
        compiler_params=params,
        name="receptor_slots",
    )(source, rec)
    tables = jnp.transpose(trans_table[dist_index], (1, 2, 0, 3))
    tables = tables.reshape(degrees, radial * dists, radial)
    one = jnp.array([members[0] for members in groups], jnp.int32)
    two = jnp.array([members[-1] for members in groups], jnp.int32)

    sums = pl.pallas_call(
        score_kernel,
        grid_spec=pltpu.PrefetchScalarGridSpec(
            num_scalar_prefetch=3,
            grid=(count,),
            in_specs=[
                pl.BlockSpec((1, radial * dists, radial), lambda i, w, one, two: (one[i], 0, 0)),
                pl.BlockSpec((1, radial * dists, radial), lambda i, w, one, two: (two[i], 0, 0)),
                pl.BlockSpec((1, 2 * deep, recs * 128), lambda i, w, one, two: (i, 0, 0)),
                pl.BlockSpec((1, half * part, 256), lambda i, w, one, two: (w[i], 0, 0)),
                pl.BlockSpec((1, half * part, 256), lambda i, w, one, two: (w[i], 0, 0)),
                pl.BlockSpec((1, rots, SLOT, 128), lambda i, w, one, two: (i, 0, 0, 0)),
                pl.BlockSpec((1, rots, SLOT, 128), lambda i, w, one, two: (i, 0, 0, 0)),
            ],
            out_specs=pl.BlockSpec((ligs, recs * dists), lambda i, w, one, two: (0, 0)),
            scratch_shapes=[
                pltpu.VMEM((radial * dists, 2 * deep), jnp.bfloat16),
                pltpu.VMEM((recs * dists, half * 256), jnp.bfloat16),
                pltpu.VMEM((2 * rots * ligs, half * 256), jnp.bfloat16),
                pltpu.VMEM((2 * rots * ligs, recs * dists), jnp.float32),
            ],
        ),
        out_shape=jax.ShapeDtypeStruct((ligs, recs * dists), jnp.float32),
        compiler_params=params,
        name="scores",
    )(where, one, two, tables, tables, rec, lig_a, lig_b, wig_a, wig_b)
    totals = jnp.sum(sums.reshape(2, part, recs, dists), axis=3)
    totals = jnp.where(core == 0, totals, totals[::-1]).reshape(ligs, recs)
    return jnp.log(totals.T)


def solution(mesh):
    in_specs = (P("rec", None, None), P("rec", None, None), P("rot", None), P(), P())
    out_specs = P("rec", "rot")
    return jax.shard_map(
        per_device, mesh=mesh, in_specs=in_specs, out_specs=out_specs, check_vma=False
    )
```

```python
import functools
import math

import jax
import jax.numpy as jnp
from jax import lax
from jax.experimental import pallas as pl
from jax.experimental.pallas import tpu as pltpu
from jax.sharding import PartitionSpec as P

SLOT = 64


def packed_start(degree):
    return degree * (4 * degree * degree - 1) // 3


def degree_groups(degrees):
    left = list(range(degrees))
    groups = []
    while left:
        members = [left.pop()]
        used = 2 * members[0] + 1
        while left:
            fits = [d for d in left if used + 2 * d + 1 <= SLOT]
            if not fits:
                break
            pick = fits[-1]
            left.remove(pick)
            members.append(pick)
            used += 2 * pick + 1
        groups.append(members)
    return groups


def column_sources(groups):
    sources = []
    for members in groups + [[]] * (len(groups) % 2):
        row = []
        for d in members:
            row += range(d * d, d * d + 2 * d + 1)
        sources += row + [-1] * (SLOT - len(row))
    return jnp.array(sources, jnp.int32)[None, :]


def select_columns(source, rows):
    shape = (rows.shape[-1], source.shape[1])
    hit = lax.broadcasted_iota(jnp.int32, shape, 0) == source
    return jnp.dot(
        rows, jnp.where(hit, 1.0, 0.0).astype(jnp.bfloat16), preferred_element_type=jnp.float32
    )


def merge_slots(first, second, group):
    lo = group // 2 * 128
    first = first[:, lo : lo + 128]
    second = second[:, lo : lo + 128]
    lane = lax.broadcasted_iota(jnp.int32, first.shape, 1)
    if group % 2:
        return jnp.where(lane < SLOT, pltpu.roll(first, SLOT, 1), second)
    return jnp.where(lane < SLOT, first, pltpu.roll(second, SLOT, 1))


def ligand_kernel(source_ref, lig_ref, out_ref):
    count, rows, _ = out_ref.shape
    slots = select_columns(source_ref[...], lig_ref[...])
    for group in range(count):
        for half in range(2):
            first = slots[half * 2 * rows : (half * 2 + 1) * rows]
            second = slots[(half * 2 + 1) * rows : (half * 2 + 2) * rows]
            merged = merge_slots(first, second, group)
            out_ref[group, :, half * 128 : (half + 1) * 128] = merged.astype(jnp.bfloat16)


def receptor_kernel(groups, depth, source_ref, rec_ref, out_ref):
    slots = select_columns(source_ref[...], rec_ref[...])
    recs = out_ref.shape[2] // 128
    lane = lax.broadcasted_iota(jnp.int32, (depth, 128), 1) % SLOT
    for group, members in enumerate(groups):
        split = 2 * members[0] + 1
        for r in range(recs):
            first = slots[2 * r * depth : (2 * r + 1) * depth]
            second = slots[(2 * r + 1) * depth : (2 * r + 2) * depth]
            merged = merge_slots(first, second, group)
            both = jnp.concatenate(
                [jnp.where(lane < split, merged, 0.0), jnp.where(lane < split, 0.0, merged)], axis=0
            )
            out_ref[group, :, r * 128 : (r + 1) * 128] = both.astype(jnp.bfloat16)


def unpack_kernel(groups, w_ref, out_ref, flat, scr):
    blocks, share, width = w_ref.shape
    rows = blocks * share
    for part in range(blocks):
        flat[part * share : (part + 1) * share, :width] = w_ref[part].astype(jnp.float32)
    lane = lax.broadcasted_iota(jnp.int32, (rows, 128), 1)
    for index, members in enumerate(groups):
        used = 0
        for d in members:
            extent = 2 * d + 1
            keep = (lane >= used) & (lane < used + extent)
            for m in range(extent):
                start = packed_start(d) + m * extent
                base = start // 128 * 128
                shift = (used - start) % 128
                window = flat[:, base : base + 128]
                if shift:
                    window = pltpu.roll(window, shift, 1)
                first = base + 128 - start
                if first < extent:
                    rest = flat[:, base + 128 : base + 256]
                    if shift:
                        rest = pltpu.roll(rest, shift, 1)
                    window = jnp.where(lane < used + first, window, rest)
                scr[:, used + m, :] = jnp.where(keep, window, 0.0)
            used += extent
        for m in range(used, SLOT):
            scr[:, m, :] = jnp.zeros((rows, 128), jnp.float32)
        out_ref[index] = scr[...].astype(jnp.bfloat16)


def unpack_wigner(wigner, groups):
    parts, share, width = wigner.shape
    rows = parts * share
    blocks = math.gcd(parts, max(16 // share, 1))
    qstep = blocks * share
    total = (width + 127) // 128 * 128 + 128
    return pl.pallas_call(
        functools.partial(unpack_kernel, groups),
        grid=(parts // blocks,),
        in_specs=[pl.BlockSpec((blocks, share, width), lambda i: (i, 0, 0))],
        out_specs=pl.BlockSpec((len(groups), qstep, SLOT, 128), lambda i: (0, i, 0, 0)),
        out_shape=jax.ShapeDtypeStruct((len(groups), rows, SLOT, 128), jnp.bfloat16),
        scratch_shapes=[
            pltpu.VMEM((qstep, total), jnp.float32),
            pltpu.VMEM((qstep, SLOT, 128), jnp.float32),
        ],
        compiler_params=pltpu.CompilerParams(vmem_limit_bytes=48 * 1024 * 1024),
        name="unpack",
    )(wigner)


def score_kernel(
    where_ref,
    one_ref,
    two_ref,
    tab_a_ref,
    tab_b_ref,
    rec_ref,
    lig_a_ref,
    lig_b_ref,
    wig_a_ref,
    wig_b_ref,
    out_ref,
    table,
    trans,
    rot,
    acc,
):
    step = pl.program_id(0)
    rots = wig_a_ref.shape[1]
    recs = rec_ref.shape[2] // 128
    rad = trans.shape[1] // 256
    dists = tab_a_ref.shape[1] // (2 * rad)
    radial = tab_a_ref.shape[2]
    part = lig_a_ref.shape[1] // rad
    ligs = 2 * part

    @pl.when(step == 0)
    def _():
        acc[...] = jnp.zeros_like(acc)
        table[...] = jnp.zeros_like(table)

    deep = table.shape[1] // 2
    table[:, :radial] = tab_a_ref[0]
    table[:, deep : deep + radial] = tab_b_ref[0]
    moved = jnp.dot(table[...], rec_ref[0], preferred_element_type=jnp.float32)
    moved = moved.reshape(2, rad, dists, recs * 128)
    for xq in range(rad):
        for half in range(2):
            piece = jnp.concatenate(
                [moved[half, xq, :, r * 128 : (r + 1) * 128] for r in range(recs)], axis=0
            )
            lo = xq * 256 + half * 128
            trans[:, lo : lo + 128] = piece.astype(jnp.bfloat16)

    low = lig_a_ref[0].astype(jnp.float32)
    high = lig_b_ref[0].astype(jnp.float32)
    rows = []
    for xq in range(rad):
        rows.append(low[xq * part : (xq + 1) * part])
        rows.append(high[xq * part : (xq + 1) * part])
    coeffs = jnp.concatenate(rows, axis=0).astype(jnp.bfloat16)
    none = jnp.zeros((2 * SLOT, 128), jnp.bfloat16)

    for source, wig_ref in enumerate((wig_a_ref, wig_b_ref)):

        def one_rotation(q, carry, wig_ref=wig_ref, source=source):
            block = wig_ref[0, q]
            other = pltpu.roll(block.astype(jnp.float32), SLOT, 1).astype(jnp.bfloat16)
            pair = jnp.concatenate([block, other], axis=0)
            full = jnp.concatenate(
                [jnp.concatenate([pair, none], axis=1), jnp.concatenate([none, pair], axis=1)],
                axis=0,
            )
            turned = jnp.dot(coeffs, full, preferred_element_type=jnp.float32).astype(jnp.bfloat16)
            row = pl.multiple_of((q + source * rots) * ligs, 16)
            for xq in range(rad):
                rot[pl.ds(row, ligs), xq * 256 : (xq + 1) * 256] = turned[
                    xq * ligs : (xq + 1) * ligs
                ]
            return carry

        lax.fori_loop(0, rots, one_rotation, 0, unroll=True)

    acc[...] += lax.dot_general(
        rot[...], trans[...], (((1,), (1,)), ((), ())), preferred_element_type=jnp.float32
    )

    @pl.when(step == pl.num_programs(0) - 1)
    def _():
        weights = jnp.exp(acc[...])
        out_ref[...] = jnp.sum(weights.reshape(2 * rots, ligs, acc.shape[1]), axis=0)


def per_device(receptors, ligands, wigner, trans_table, dist_index):
    degrees = trans_table.shape[1]
    radial = trans_table.shape[2]
    half = radial // 2
    groups = degree_groups(degrees)
    count = len(groups)
    padded = count + count % 2
    source = column_sources(groups)
    recs, rows, angular = receptors.shape
    props = rows // radial
    dists = dist_index.shape[0]
    nrec = lax.axis_size("rec")
    part = ligands.shape[0]
    ligs = 2 * part
    params = pltpu.CompilerParams(vmem_limit_bytes=48 * 1024 * 1024)
    core = lax.axis_index("rec") % 2
    swap = [(i, i ^ 1) for i in range(nrec)]
    same_core = [list(range(c, nrec, 2)) for c in range(2)]

    share = wigner.shape[0] // 2
    own = lax.dynamic_slice_in_dim(wigner, core * share, share, 0)
    turns_a = lax.all_gather(own, "rot", axis=0)
    turns_b = lax.ppermute(turns_a, "rec", swap)
    rots = turns_a.shape[0] * share

    lig = ligands.reshape(part, props, 2, half, angular)
    lig = jnp.transpose(lig, (2, 1, 3, 0, 4)).reshape(4 * half * part, angular)
    lig = pl.pallas_call(
        ligand_kernel,
        out_shape=jax.ShapeDtypeStruct((padded, half * part, 256), jnp.bfloat16),
        compiler_params=params,
        name="ligand_slots",
    )(source, lig)
    pieces = lig.reshape(nrec // 2, -1, 256)
    spread = lax.all_to_all(pieces, "rec", 0, 0, axis_index_groups=same_core)

    deep = (radial + 15) // 16 * 16
    rec = receptors.reshape(recs * props, radial, angular)
    rec = jnp.pad(rec, ((0, 0), (0, deep - radial), (0, 0))).reshape(-1, angular)
    rec = pl.pallas_call(
        functools.partial(receptor_kernel, groups, deep),
        out_shape=jax.ShapeDtypeStruct((count, 2 * deep, recs * 128), jnp.bfloat16),
        compiler_params=params,
        name="receptor_slots",
    )(source, rec)
    tables = jnp.transpose(trans_table[dist_index], (1, 2, 0, 3))
    tables = tables.reshape(degrees, radial * dists, radial)
    spread, rec, tables = lax.optimization_barrier((spread, rec, tables))
    mine = lax.dynamic_index_in_dim(spread, lax.axis_index("rot"), 0, keepdims=False)
    found = [mine]
    for k in range(1, nrec // 2):
        found.append(lax.ppermute(mine, "rec", [(i, i ^ (2 * k)) for i in range(nrec)]))
    lig_a = jnp.concatenate(found, axis=0).reshape(padded, half * part, 256)
    lig_b = lax.ppermute(lig_a, "rec", swap)
    each = padded // (nrec // 2)
    order = jnp.arange(count, dtype=jnp.int32)
    chip = (lax.axis_index("rec") // 2).astype(jnp.int32)
    where = (chip ^ (order // each)) * each + order % each

    wig_a = unpack_wigner(turns_a, groups)
    wig_b = unpack_wigner(turns_b, groups)

    one = jnp.array([members[0] for members in groups], jnp.int32)
    two = jnp.array([members[-1] for members in groups], jnp.int32)

    sums = pl.pallas_call(
        score_kernel,
        grid_spec=pltpu.PrefetchScalarGridSpec(
            num_scalar_prefetch=3,
            grid=(count,),
            in_specs=[
                pl.BlockSpec((1, radial * dists, radial), lambda i, w, one, two: (one[i], 0, 0)),
                pl.BlockSpec((1, radial * dists, radial), lambda i, w, one, two: (two[i], 0, 0)),
                pl.BlockSpec((1, 2 * deep, recs * 128), lambda i, w, one, two: (i, 0, 0)),
                pl.BlockSpec((1, half * part, 256), lambda i, w, one, two: (w[i], 0, 0)),
                pl.BlockSpec((1, half * part, 256), lambda i, w, one, two: (w[i], 0, 0)),
                pl.BlockSpec((1, rots, SLOT, 128), lambda i, w, one, two: (i, 0, 0, 0)),
                pl.BlockSpec((1, rots, SLOT, 128), lambda i, w, one, two: (i, 0, 0, 0)),
            ],
            out_specs=pl.BlockSpec((ligs, recs * dists), lambda i, w, one, two: (0, 0)),
            scratch_shapes=[
                pltpu.VMEM((radial * dists, 2 * deep), jnp.bfloat16),
                pltpu.VMEM((recs * dists, half * 256), jnp.bfloat16),
                pltpu.VMEM((2 * rots * ligs, half * 256), jnp.bfloat16),
                pltpu.VMEM((2 * rots * ligs, recs * dists), jnp.float32),
            ],
        ),
        out_shape=jax.ShapeDtypeStruct((ligs, recs * dists), jnp.float32),
        compiler_params=params,
        name="scores",
    )(where, one, two, tables, tables, rec, lig_a, lig_b, wig_a, wig_b)
    totals = jnp.sum(sums.reshape(2, part, recs, dists), axis=3)
    totals = jnp.where(core == 0, totals, totals[::-1]).reshape(ligs, recs)
    return jnp.log(totals.T)


def solution(mesh):
    in_specs = (P("rec", None, None), P("rec", None, None), P("rot", None), P(), P())
    out_specs = P("rec", "rot")
    return jax.shard_map(
        per_device, mesh=mesh, in_specs=in_specs, out_specs=out_specs, check_vma=False
    )
```
